256 devices in a mesh: row: 16 (over x_lo, z), col: 16 (over y, x_hi, core).
Axes of the slice: x: 4 (x_hi: 2, x_lo: 2; x = x_hi * 2 + x_lo), y: 4, z: 8, core: 2. Of those that a mesh axis runs over, the one named last changes fastest.
Arguments:
- features: bfloat16 [524288, 128], P(('col', 'row')), may hold values from -6 to 6
- weight: bfloat16 [128, 128], replicated, may hold values from -0.5 to 0.5
- tile_row: int32 [262144], P(('row', 'col')), may hold values from 0 to 255
- tile_col: int32 [262144], P(('row', 'col')), may hold values from 0 to 255
- tile_count: int32 [256], P(('row', 'col')), may hold values from 256 to 1024, as said below
- edge_row: int32 [262144, 64], P(('row', 'col')), may hold values from 0 to 127, as said below
- edge_col: int32 [262144, 64], P(('row', 'col')), may hold values from 0 to 127
- edge_weight: bfloat16 [262144, 64], P(('row', 'col')), may hold values from 0.049804688 to 0.5
Outputs:
- activated: bfloat16 [524288, 128], P(('row', 'col'))
The draws below stay inside these ranges and needn't reach their ends.
Inputs may be any that keep to these rules, and one draw needn't show every extreme that they name: The first tile_count[d] slots of a device hold its nonzero tiles, at distinct positions and in increasing order of (tile_row, tile_col); exactly one device fills all 1024 slots; later slots are unused. `edge_row`: the 64 edges of a tile lie at distinct positions of the tile.
All inputs are finite; a program needn't handle non-finite values.
Results may differ from the reference program's by a relative error of at most 0.0049.
Values may be sent and summed in bfloat16 or wider, within the bound.
A program may use at most 128 MiB of HBM per device.

```python
import math
import jax
import jax.numpy as jnp
from jax import lax

HIDDEN_SIZE = 128
TILE = 128
EDGES = 64
NODE_DEV = 2048
NODES = 524288
TROWS = 256
TCOLS = 256
TILES_DEV = 1024
N_ROW = 16
N_COL = 16


def tile_layout(key):
    device_total = N_ROW * N_COL
    key_count, key_top, key_offset = jax.random.split(key, 3)
    counts = jax.random.randint(key_count, (device_total,), TILES_DEV // 4, TILES_DEV).astype(jnp.int32)
    top = jax.random.randint(key_top, (), 0, device_total)
    counts = jnp.where(jnp.arange(device_total) == top, TILES_DEV, counts).astype(jnp.int32)
    positions = TROWS * TCOLS
    stride = positions // counts
    slots = jnp.arange(TILES_DEV, dtype=jnp.int32)
    offsets = jax.random.randint(key_offset, (device_total, TILES_DEV), 0, 2 ** 30) % stride[:, None]
    flat = slots[None, :] * stride[:, None] + offsets
    flat = jnp.where(slots[None, :] < counts[:, None], flat, offsets % positions)
    return (counts, flat.astype(jnp.int32))


def edge_layout(key):
    tiles_all = N_ROW * N_COL * TILES_DEV
    key_mult, key_shift, key_pick = jax.random.split(key, 3)
    area = TILE * TILE
    span = area // EDGES
    mult = 2 * jax.random.randint(key_mult, (tiles_all, 1), 0, area // 2) + 1
    shift = jax.random.randint(key_shift, (tiles_all, 1), 0, area)
    picks = jax.random.randint(key_pick, (tiles_all, EDGES), 0, span)
    base = jnp.arange(EDGES, dtype=jnp.int32)[None, :] * span + picks
    return ((mult * base + shift) % area).astype(jnp.int32)


def draw_tile_row(key, part):
    counts, flat = tile_layout(key)
    return (flat // TCOLS).reshape(-1).astype(jnp.int32)


def draw_tile_col(key, part):
    counts, flat = tile_layout(key)
    return (flat % TCOLS).reshape(-1).astype(jnp.int32)


def draw_tile_count(key, part):
    counts, flat = tile_layout(key)
    return counts


def draw_edge_row(key, part):
    return edge_layout(jax.random.fold_in(key, 11)) // TILE


def draw_edge_col(key, part):
    return edge_layout(jax.random.fold_in(key, 11)) % TILE


def levels(key, shape, cuts, smallest, largest):
    loudness = 1.0
    for dim, blocks in cuts:
        steps = jax.random.uniform(jax.random.fold_in(jax.random.fold_in(key, 6), dim), (blocks,), jnp.float32, smallest / len(cuts), largest / len(cuts))
        loudness = loudness * jnp.repeat(jnp.exp(steps), shape[dim] // blocks).reshape((-1,) + (1,) * (len(shape) - 1 - dim))
    return loudness


def bell_draw(own_key, extent, deviation, reach, cuts=(), kind=jnp.bfloat16):
    entries = deviation * jax.random.normal(own_key, extent, jnp.float32)
    if cuts:
        entries = entries * levels(own_key, extent, cuts, -0.22, 0.18)
    return jnp.clip(entries, -reach, reach).astype(kind)


def setup_inputs(seed: int = 0) -> dict:
    key_of = jax.random.split(jax.random.key(seed), 9)
    features = bell_draw(key_of[0], (NODES, HIDDEN_SIZE), 1.0, 6.0, ((0, 256),))
    weight = bell_draw(key_of[1], (HIDDEN_SIZE, HIDDEN_SIZE), HIDDEN_SIZE ** -0.5, 0.5)
    tile_row = draw_tile_row(jax.random.fold_in(key_of[8], 71), 0)
    tile_col = draw_tile_col(jax.random.fold_in(key_of[8], 71), 0)
    tile_count = draw_tile_count(jax.random.fold_in(key_of[8], 71), 0)
    edge_row = draw_edge_row(jax.random.fold_in(key_of[8], 71), 0)
    edge_col = draw_edge_col(jax.random.fold_in(key_of[8], 71), 0)
    edge_weight = jnp.clip(jnp.exp(math.log(0.5) - 2.306499 * jax.random.uniform(key_of[7], (N_ROW * N_COL * TILES_DEV, EDGES), jnp.float32) ** levels(key_of[7], (N_ROW * N_COL * TILES_DEV, EDGES), ((0, 256),), -0.2, 0.2)), 0.049804688, 0.5).astype(jnp.bfloat16)
    return {"features": features, "weight": weight, "tile_row": tile_row, "tile_col": tile_col, "tile_count": tile_count, "edge_row": edge_row, "edge_col": edge_col, "edge_weight": edge_weight}


def reference(features, weight, tile_row, tile_col, tile_count, edge_row, edge_col, edge_weight):
    device_total = N_ROW * N_COL
    transformed = jnp.dot(features, weight, preferred_element_type=jnp.float32).astype(jnp.bfloat16)
    rows_all = tile_row.reshape(device_total, TILES_DEV)
    cols_all = tile_col.reshape(device_total, TILES_DEV)
    erow_all = edge_row.reshape(device_total, TILES_DEV, EDGES)
    ecol_all = edge_col.reshape(device_total, TILES_DEV, EDGES)
    wgt_all = edge_weight.reshape(device_total, TILES_DEV, EDGES)

    def add_device(total, index):
        r_index = index // N_COL
        c_index = index % N_COL
        targets = (r_index * (N_COL * NODE_DEV) + rows_all[index][:, None] * TILE + erow_all[index]).astype(jnp.int32)
        sources = (c_index * (N_ROW * NODE_DEV) + cols_all[index][:, None] * TILE + ecol_all[index]).astype(jnp.int32)
        live = jnp.arange(TILES_DEV, dtype=jnp.int32) < tile_count[index]
        weights = jnp.where(live[:, None], wgt_all[index].astype(jnp.float32), jnp.float32(0.0))
        message = weights[:, :, None] * transformed[sources.reshape(-1)].astype(jnp.float32).reshape(TILES_DEV, EDGES, HIDDEN_SIZE)
        total = total.at[targets.reshape(-1)].add(message.reshape(-1, HIDDEN_SIZE))
        return total, None

    start = jnp.zeros((NODE_DEV * N_ROW * N_COL, HIDDEN_SIZE), jnp.float32)
    aggregated, unused = lax.scan(add_device, start, jnp.arange(device_total, dtype=jnp.int32))
    return jnp.maximum(aggregated, jnp.float32(0.0)).astype(jnp.bfloat16)
```

```python
import jax
import jax.numpy as jnp
from jax import lax
from jax.experimental import pallas as pl
from jax.experimental.pallas import tpu as pltpu
from jax.sharding import PartitionSpec as P

MESH = pl.DeviceIdType.MESH
BF, F32 = jnp.bfloat16, jnp.float32

TILE = 128
FEAT = 128
NODE = 2048
SLOTS = 1024
HALF = SLOTS // 2
EDGES = 64
ZN, YN = 8, 4
NT = NODE // TILE
EARLY = 7
LATE = NT - EARLY
HALVES = {1: (EARLY, LATE // 2), -1: (EARLY + LATE // 2, LATE - LATE // 2)}
PIECES = 4
PROWS = NODE // PIECES
X_FIRST = (False, True, False, True)
MIB = 2**20


def place():
    row, col = lax.axis_index("row"), lax.axis_index("col")
    return row // ZN, row % ZN, col // 4, (col // 2) % 2, col % 2


def device(xlo, z, y, xhi, core):
    return (xlo * ZN + z, y * 4 + xhi * 2 + core)


def add_rows(dst, dst_row, parts, rows, finish=None):
    step = 128

    def body(i, carry):
        total = None
        for ref, first in parts:
            term = ref[pl.ds(pl.multiple_of(first + i * step, 64), step), :].astype(F32)
            total = term if total is None else total + term
        if finish is not None:
            total = finish(total)
        dst[pl.ds(pl.multiple_of(dst_row + i * step, 64), step), :] = total.astype(BF)
        return carry

    lax.fori_loop(0, rows // step, body, 0, unroll=2)


def layer_kernel(
    tile_row, tile_col, ends,
    feat, weight, edge_row, edge_col, edge_weight,
    out,
    x, tiles, er2, ec2, ew2, acc, give, mine, got,
    y_in, yx_in, xy_in, x_in,
    send, recv,
):
    xlo, z, y, xhi, core = place()
    z_next = {1: device(xlo, (z + 1) % ZN, y, xhi, core), -1: device(xlo, (z + ZN - 1) % ZN, y, xhi, core)}
    y_next = {1: device(xlo, z, (y + 1) % YN, xhi, core), -1: device(xlo, z, (y + YN - 1) % YN, xhi, core)}
    x_pair = device(1 - xlo, z, y, xhi, core)
    x_far = device(xlo, z, y, 1 - xhi, core)
    sibling = device(xlo, z, y, xhi, 1 - core)

    barrier = pltpu.get_barrier_semaphore()
    others = [z_next[1], z_next[-1], y_next[1], y_next[-1], x_pair, x_far, sibling]
    for other in others:
        pl.semaphore_signal(barrier, inc=1, device_id=other, device_id_type=MESH)

    copies = []

    def start(src, dst, target):
        number = len(copies)
        copy = pltpu.make_async_remote_copy(
            src_ref=src, dst_ref=dst, send_sem=send.at[number], recv_sem=recv.at[number],
            device_id=target, device_id_type=MESH,
        )
        copy.start()
        copies.append(copy)
        return copy

    def block(i, zz):
        return (i * ZN + zz) * NT

    own = block(xlo, z)

    def transform(i, carry):
        rows = pl.ds(pl.multiple_of(i * 256, 256), 256)
        part = jnp.dot(feat[rows, :], weight[...], preferred_element_type=F32).astype(BF)
        x[pl.ds(own + i * 2, 2)] = part.reshape(2, TILE, FEAT)
        return carry

    lax.fori_loop(0, NODE // 256, transform, 0)

    lane = lax.broadcasted_iota(jnp.int32, (16, 128), 1)
    shift = jnp.where(lane >= EDGES, 128.0, 0.0)

    def prep(i, carry):
        first = pl.multiple_of(i * 16, 16)
        rows, later = pl.ds(first, 16), pl.ds(pl.multiple_of(first + HALF, 16), 16)

        def both(ref):
            return jnp.concatenate([ref[rows, :], ref[later, :]], axis=1).astype(F32)

        er2[rows, :] = both(edge_row)
        ec2[rows, :] = both(edge_col) + shift
        ew = jnp.concatenate([edge_weight[rows, :].astype(F32), edge_weight[later, :].astype(F32)], axis=1)
        ew2[rows, :] = ew
        return carry

    iota = lax.broadcasted_iota(jnp.int32, (256, 128), 0).astype(F32).astype(BF)
    GROUP = 4

    def build(i, carry):
        for u in range(GROUP):
            p = i * GROUP + u

            def spread(ref, n):
                return jnp.concatenate([jnp.broadcast_to(ref[pl.ds(p, 1), :], (16, 128)).astype(BF)] * n, axis=0)

            picks = jnp.where(spread(er2, 8) == iota[:128], spread(ew2, 8), jnp.zeros((128, 128), BF))
            sources = jnp.where(spread(ec2, 16) == iota, jnp.ones((256, 128), BF), jnp.zeros((256, 128), BF))
            dense = lax.dot_general(picks, sources, (((1,), (1,)), ((), ())), preferred_element_type=F32).astype(BF)
            tiles[p] = dense[:, :128]
            tiles[p + HALF] = dense[:, 128:]
        return carry

    built = [0]

    def build_some(n):
        first = built[0]
        lax.fori_loop(first, first + n, build, 0)
        built[0] = first + n

    def rows_of(i, zz, offset, n):
        return x.at[pl.ds(block(i, zz) + offset, n)]

    def ring(direction, hop, i, offset, n):
        ref = rows_of(i, (z - direction * (hop - 1) + ZN) % ZN, offset, n)
        return start(ref, ref, z_next[direction])

    def cross(direction, hop, offset, n):
        ref = rows_of(xlo, (z - direction * hop + ZN) % ZN, offset, n)
        return start(ref, ref, x_pair)

    late, early, pair_early = (xlo, EARLY, LATE), (xlo, 0, EARLY), (1 - xlo, 0, EARLY)
    pl.semaphore_wait(barrier, len(others))
    hops = {}
    for d in (1, -1):
        hops[1, d, "late"] = ring(d, 1, *late)
    cross_early = cross(1, 0, 0, EARLY)
    for d in (1, -1):
        hops[1, d, "early"] = ring(d, 1, *early)
    crossed = [cross(1, 0, EARLY, LATE)]
    lax.fori_loop(0, HALF // 16, prep, 0)
    build_some(8)
    cross_early.wait_recv()
    for d in (1, -1):
        hops[1, d, "pair"] = ring(d, 1, *pair_early)
    final = []
    for hop in (1, 2, 3):
        for name, part in (("late", late), ("early", early), ("pair", pair_early)):
            build_some(12)
            for d in (1, -1):
                hops[hop, d, name].wait_recv()
                if hop < 3:
                    hops[hop + 1, d, name] = ring(d, hop + 1, *part)
                elif name == "late":
                    hops[4, d, name] = ring(d, 4, xlo, *HALVES[d])
                elif (name == "early") == (d == 1):
                    final.append(ring(d, 4, *part))
                if name == "late":
                    crossed.append(cross(d, hop, EARLY, LATE))
    build_some(HALF // GROUP - built[0])
    for d in (1, -1):
        hops[4, d, "late"].wait_recv()
        crossed.append(cross(d, 4, *HALVES[d]))
    for copy in final + crossed:
        copy.wait_recv()

    acc[...] = jnp.zeros_like(acc)
    STEP = 8

    def accumulate(i, carry):
        products = []
        for u in range(STEP):
            s = i * STEP + u
            products.append(jnp.dot(tiles[s], x[tile_col[s]], preferred_element_type=F32))
        total = acc[...]
        for u in range(STEP):
            s = i * STEP + u
            step = tile_row[s] - tile_row[jnp.maximum(s - 1, 0)]
            keep = jnp.maximum(1 - jnp.maximum(step, 0), 0).astype(F32)
            total = total * keep + products[u]
            tiles[s] = total.astype(BF)
        acc[...] = total
        return carry

    lax.fori_loop(0, SLOTS // STEP, accumulate, 0)

    def emit(buffer, owner_core, j):
        def body(q, carry):
            xx, yy = q // YN, q % YN
            first = (yy * 4 + xx * 2 + owner_core) * (NODE // TILE) + j * (PROWS // TILE)
            for g in range(PROWS // TILE):
                end = ends[first + g + 1]
                found = jnp.minimum(end - ends[first + g], 1).astype(F32)
                total = tiles[jnp.maximum(end - 1, 0)] * jnp.full((TILE, FEAT), found, F32).astype(BF)
                buffer[j, pl.ds(pl.multiple_of(q * PROWS + g * TILE, TILE), TILE), :] = total
            return carry

        lax.fori_loop(0, 2 * YN, body, 0)

    given = []
    for j in range(PIECES):
        emit(give, 1 - core, j)
        given.append(start(give.at[j], got.at[j], sibling))
    for j in range(PIECES):
        emit(mine, core, j)

    def chunk(xx, yy):
        return (xx * YN + yy) * PROWS

    def at(ref, first, n):
        return ref.at[pl.ds(pl.multiple_of(first, 64), n)]

    up, down, far = (y + 1) % YN, (y + YN - 1) % YN, (y + 2) % YN
    h = PROWS // 2
    state = [None] * PIECES
    slot = {j: n for kind in (False, True) for n, j in enumerate([k for k in range(PIECES) if X_FIRST[k] == kind])}
    for j in range(PIECES):
        given[j].wait_recv()
        sums, land = mine.at[j], slot[j]
        add_rows(sums, 0, [(sums, 0), (got.at[j], 0)], 2 * YN * PROWS)
        if X_FIRST[j]:
            state[j] = start(at(sums, chunk(1 - xhi, 0), YN * PROWS), x_in.at[land], x_far)
        else:
            into = y_in.at[land]
            state[j] = [
                start(at(sums, chunk(0, far), PROWS), at(into, 0, PROWS), y_next[1]),
                start(at(sums, chunk(1, far), PROWS), at(into, PROWS, PROWS), y_next[-1]),
                start(at(sums, chunk(1, up), PROWS), at(into, 2 * PROWS, PROWS), y_next[1]),
                start(at(sums, chunk(0, down), PROWS), at(into, 3 * PROWS, PROWS), y_next[-1]),
            ]
    for j in range(PIECES):
        sums, land = mine.at[j], slot[j]
        if X_FIRST[j]:
            state[j].wait_recv()
            into, base = xy_in.at[land], chunk(xhi, 0)
            add_rows(sums, base, [(sums, base), (x_in.at[land], 0)], YN * PROWS)
            state[j] = [
                start(at(sums, chunk(xhi, far), h), at(into, 0, h), y_next[1]),
                start(at(sums, chunk(xhi, far) + h, h), at(into, h, h), y_next[-1]),
                start(at(sums, chunk(xhi, up) + h, h), at(into, 2 * h, h), y_next[1]),
                start(at(sums, chunk(xhi, down), h), at(into, 3 * h, h), y_next[-1]),
            ]
        else:
            into = y_in.at[land]
            state[j][0].wait_recv()
            add_rows(sums, chunk(0, up), [(sums, chunk(0, up)), (into, 0)], PROWS)
            state[j].append(start(at(sums, chunk(0, up), PROWS), at(into, 4 * PROWS, PROWS), y_next[1]))
            state[j][1].wait_recv()
            add_rows(sums, chunk(1, down), [(sums, chunk(1, down)), (into, PROWS)], PROWS)
            state[j].append(start(at(sums, chunk(1, down), PROWS), at(into, 5 * PROWS, PROWS), y_next[-1]))
    for j in range(PIECES):
        sums, land = mine.at[j], slot[j]
        if X_FIRST[j]:
            into = xy_in.at[land]
            state[j][0].wait_recv()
            add_rows(sums, chunk(xhi, up), [(sums, chunk(xhi, up)), (into, 0)], h)
            state[j].append(start(at(sums, chunk(xhi, up), h), at(into, 4 * h, h), y_next[1]))
            state[j][1].wait_recv()
            add_rows(sums, chunk(xhi, down) + h, [(sums, chunk(xhi, down) + h), (into, h)], h)
            state[j].append(start(at(sums, chunk(xhi, down) + h, h), at(into, 5 * h, h), y_next[-1]))
        else:
            into = y_in.at[land]
            for copy in state[j][2:]:
                copy.wait_recv()
            low = (4, 3)
            high = (2, 5)
            for xx, (one, two) in ((0, low), (1, high)):
                add_rows(
                    sums, chunk(xx, y), [(sums, chunk(xx, y)), (into, one * PROWS), (into, two * PROWS)], PROWS
                )
            state[j] = start(at(sums, chunk(1 - xhi, y), PROWS), yx_in.at[land], x_far)
    relu = lambda v: jnp.maximum(v, 0.0)
    for j in range(PIECES):
        sums, land = mine.at[j], slot[j]
        if X_FIRST[j]:
            into, base = xy_in.at[land], chunk(xhi, y)
            for copy in state[j][2:]:
                copy.wait_recv()
            add_rows(out, j * PROWS, [(sums, base), (into, 4 * h), (into, 3 * h)], h, relu)
            add_rows(out, j * PROWS + h, [(sums, base + h), (into, 2 * h), (into, 5 * h)], h, relu)
        else:
            state[j].wait_recv()
            add_rows(out, j * PROWS, [(sums, chunk(xhi, y)), (yx_in.at[land], 0)], PROWS, relu)
    for copy in copies:
        copy.wait_send()


def local(features, weight, tile_row, tile_col, tile_count, edge_row, edge_col, edge_weight):
    live = jnp.arange(SLOTS, dtype=jnp.int32) < tile_count[0]
    starts = jnp.arange(257, dtype=jnp.int32)
    ends = jnp.sum(((tile_row[None, :] < starts[:, None]) & live[None, :]).astype(jnp.int32), axis=1)
    smem = pl.BlockSpec(memory_space=pltpu.SMEM)
    vmem = pl.BlockSpec(memory_space=pltpu.VMEM)
    n_y, n_x = X_FIRST.count(False), X_FIRST.count(True)
    copies = 64 + 8 * PIECES
    return pl.pallas_call(
        layer_kernel,
        out_shape=jax.ShapeDtypeStruct((NODE, FEAT), BF),
        in_specs=[smem] * 3 + [vmem] * 5,
        out_specs=vmem,
        scratch_shapes=[
            pltpu.VMEM((16 * NT, TILE, FEAT), BF),
            pltpu.VMEM((SLOTS, TILE, FEAT), BF),
            pltpu.VMEM((HALF, 128), F32),
            pltpu.VMEM((HALF, 128), F32),
            pltpu.VMEM((HALF, 128), F32),
            pltpu.VMEM((TILE, FEAT), F32),
            pltpu.VMEM((PIECES, 2 * YN * PROWS, FEAT), BF),
            pltpu.VMEM((PIECES, 2 * YN * PROWS, FEAT), BF),
            pltpu.VMEM((PIECES, 2 * YN * PROWS, FEAT), BF),
            pltpu.VMEM((n_y, 6 * PROWS, FEAT), BF),
            pltpu.VMEM((n_y, PROWS, FEAT), BF),
            pltpu.VMEM((n_x, 3 * PROWS, FEAT), BF),
            pltpu.VMEM((n_x, YN * PROWS, FEAT), BF),
            pltpu.SemaphoreType.DMA((copies,)),
            pltpu.SemaphoreType.DMA((copies,)),
        ],
        compiler_params=pltpu.CompilerParams(
            collective_id=0, has_side_effects=True, vmem_limit_bytes=62 * MIB
        ),
        cost_estimate=pl.CostEstimate(flops=9 * 10**9, bytes_accessed=4 * MIB, transcendentals=0),
        name="graph_layer",
    )(tile_row, tile_col, ends, features, weight, edge_row, edge_col, edge_weight)


def solution(mesh):
    in_specs = (
        P(("col", "row"), None),
        P(),
        P(("row", "col")),
        P(("row", "col")),
        P(("row", "col")),
        P(("row", "col"), None),
        P(("row", "col"), None),
        P(("row", "col"), None),
    )
    out_specs = P(("row", "col"), None)
    return jax.shard_map(local, mesh=mesh, in_specs=in_specs, out_specs=out_specs, check_vma=False)
```

```python
import jax
import jax.numpy as jnp
from jax import lax
from jax.experimental import pallas as pl
from jax.experimental.pallas import tpu as pltpu
from jax.sharding import PartitionSpec as P

MESH = pl.DeviceIdType.MESH
BF, F32 = jnp.bfloat16, jnp.float32

TILE = 128
FEAT = 128
NODE = 2048
SLOTS = 1024
ENDS = 260
HALF = SLOTS // 2
EDGES = 64
ZN, YN = 8, 4
NT = NODE // TILE
EARLY = 7
LATE = NT - EARLY
HALVES = {1: (EARLY, LATE // 2), -1: (EARLY + LATE // 2, LATE - LATE // 2)}
PIECES = 8
PROWS = NODE // PIECES
X_FIRST = (True, False, True, False, True, False, False, False)
AHEAD = 2
FIRSTS = (0, 1, 2, 3, 4, 5, 6, 7)
LATER = (1, 3, 5, 6, 7, 0, 2, 4)
MIB = 2**20


def place():
    row, col = lax.axis_index("row"), lax.axis_index("col")
    return row // ZN, row % ZN, col // 4, (col // 2) % 2, col % 2


def device(xlo, z, y, xhi, core):
    return (xlo * ZN + z, y * 4 + xhi * 2 + core)


def add_rows(dst, dst_row, parts, rows, finish=None):
    step = min(rows, 512)

    def body(i, carry):
        total = None
        for ref, first in parts:
            term = ref[pl.ds(pl.multiple_of(first + i * step, 64), step), :].astype(F32)
            total = term if total is None else total + term
        if finish is not None:
            total = finish(total)
        dst[pl.ds(pl.multiple_of(dst_row + i * step, 64), step), :] = total.astype(BF)
        return carry

    lax.fori_loop(0, rows // step, body, 0)


def layer_kernel(
    tile_row, tile_col, count_ref,
    feat, weight, edge_row, edge_col, edge_weight,
    out,
    x, tiles, er2, ec2, ew2, acc, give, mine, got,
    y_in, yx_in, xy_in, x_in,
    ends, send, recv,
):
    xlo, z, y, xhi, core = place()
    z_next = {1: device(xlo, (z + 1) % ZN, y, xhi, core), -1: device(xlo, (z + ZN - 1) % ZN, y, xhi, core)}
    y_next = {1: device(xlo, z, (y + 1) % YN, xhi, core), -1: device(xlo, z, (y + YN - 1) % YN, xhi, core)}
    x_pair = device(1 - xlo, z, y, xhi, core)
    x_far = device(xlo, z, y, 1 - xhi, core)
    sibling = device(xlo, z, y, xhi, 1 - core)

    barrier = pltpu.get_barrier_semaphore()
    others = [z_next[1], z_next[-1], y_next[1], y_next[-1], x_pair, x_far, sibling]
    for other in others:
        pl.semaphore_signal(barrier, inc=1, device_id=other, device_id_type=MESH)

    copies = []

    def start(src, dst, target):
        number = len(copies)
        copy = pltpu.make_async_remote_copy(
            src_ref=src, dst_ref=dst, send_sem=send.at[number], recv_sem=recv.at[number],
            device_id=target, device_id_type=MESH,
        )
        copy.start()
        copies.append(copy)
        return copy

    def block(i, zz):
        return (i * ZN + zz) * NT

    own = block(xlo, z)

    def transform(i, carry):
        rows = pl.ds(pl.multiple_of(i * 256, 256), 256)
        part = jnp.dot(feat[rows, :], weight[...], preferred_element_type=F32).astype(BF)
        x[pl.ds(own + i * 2, 2)] = part.reshape(2, TILE, FEAT)
        return carry

    lax.fori_loop(0, NODE // 256, transform, 0)

    def prep(i, carry):
        rows = pl.ds(pl.multiple_of(i * 128, 128), 128)

        def both(ref):
            first = ref[:, pl.ds(pl.multiple_of(i * 128, 128), 128)].astype(F32)
            later = ref[:, pl.ds(pl.multiple_of(i * 128 + HALF, 128), 128)].astype(F32)
            return first, later

        first, later = both(edge_row)
        er2[rows, :] = jnp.concatenate([first, later], axis=0).T
        first, later = both(edge_col)
        ec2[rows, :] = jnp.concatenate([first, later + 128.0], axis=0).T
        first, later = both(edge_weight)
        ew2[rows, :] = jnp.concatenate([first, later], axis=0).T
        return carry

    iota = lax.broadcasted_iota(jnp.int32, (256, 128), 0).astype(F32).astype(BF)
    GROUP = 4

    def build(i, carry):
        for u in range(GROUP):
            p = i * GROUP + u

            def spread(ref, n):
                return jnp.concatenate([jnp.broadcast_to(ref[pl.ds(p, 1), :], (16, 128)).astype(BF)] * n, axis=0)

            picks = jnp.where(spread(er2, 8) == iota[:128], spread(ew2, 8), jnp.zeros((128, 128), BF))
            sources = jnp.where(spread(ec2, 16) == iota, jnp.ones((256, 128), BF), jnp.zeros((256, 128), BF))
            dense = lax.dot_general(picks, sources, (((1,), (1,)), ((), ())), preferred_element_type=F32).astype(BF)
            tiles[p] = dense[:, :128]
            tiles[p + HALF] = dense[:, 128:]
        return carry

    count = count_ref[0]
    ROWS_AT_ONCE = 4

    def unit(v):
        return jnp.minimum(jnp.maximum(v, 0), 1)

    def bisect(i, carry):
        rows = [i * ROWS_AT_ONCE + u for u in range(ROWS_AT_ONCE)]
        found = [i * 0 for row in rows]
        for step in (512, 256, 128, 64, 32, 16, 8, 4, 2, 1, 1):
            for u, row in enumerate(rows):
                probe = found[u] + step
                below = unit(row - tile_row[jnp.minimum(probe, SLOTS) - 1])
                found[u] = found[u] + step * below * unit(count + 1 - probe)
        for u, row in enumerate(rows):
            ends[row] = found[u]
        return carry

    bisected = [0]

    def bisect_some(n):
        first = bisected[0]
        lax.fori_loop(first, min(first + n, ENDS // ROWS_AT_ONCE), bisect, 0)
        bisected[0] = min(first + n, ENDS // ROWS_AT_ONCE)

    built = [0]

    def build_some(n):
        first = built[0]
        lax.fori_loop(first, first + n, build, 0)
        built[0] = first + n

    def rows_of(i, zz, offset, n):
        return x.at[pl.ds(block(i, zz) + offset, n)]

    def ring(direction, hop, i, offset, n):
        ref = rows_of(i, (z - direction * (hop - 1) + ZN) % ZN, offset, n)
        return start(ref, ref, z_next[direction])

    def cross(direction, hop, offset, n):
        ref = rows_of(xlo, (z - direction * hop + ZN) % ZN, offset, n)
        return start(ref, ref, x_pair)

    late, early, pair_early = (xlo, EARLY, LATE), (xlo, 0, EARLY), (1 - xlo, 0, EARLY)
    pl.semaphore_wait(barrier, len(others))
    hops = {}
    for d in (1, -1):
        hops[1, d, "late"] = ring(d, 1, *late)
    cross_early = cross(1, 0, 0, EARLY)
    for d in (1, -1):
        hops[1, d, "early"] = ring(d, 1, *early)
    crossed = [cross(1, 0, EARLY, LATE)]
    lax.fori_loop(0, HALF // 128, prep, 0)
    build_some(8)
    cross_early.wait_recv()
    for d in (1, -1):
        hops[1, d, "pair"] = ring(d, 1, *pair_early)
    final = []
    for hop in (1, 2, 3):
        for name, part in (("late", late), ("early", early), ("pair", pair_early)):
            build_some(12)
            bisect_some(8)
            for d in (1, -1):
                hops[hop, d, name].wait_recv()
                if hop < 3:
                    hops[hop + 1, d, name] = ring(d, hop + 1, *part)
                elif name == "late":
                    hops[4, d, name] = ring(d, 4, xlo, *HALVES[d])
                elif (name == "early") == (d == 1):
                    final.append(ring(d, 4, *part))
                if name == "late":
                    crossed.append(cross(d, hop, EARLY, LATE))
    build_some(HALF // GROUP - built[0])
    for d in (1, -1):
        hops[4, d, "late"].wait_recv()
        crossed.append(cross(d, 4, *HALVES[d]))
    for copy in final + crossed:
        copy.wait_recv()

    acc[...] = jnp.zeros_like(acc)
    STEP = 64

    def accumulate(i, carry):
        products = []
        for u in range(STEP):
            s = i * STEP + u
            products.append(jnp.dot(tiles[s], x[tile_col[s]], preferred_element_type=F32))
        total = acc[...]
        for u in range(STEP):
            s = i * STEP + u
            step = tile_row[s] - tile_row[jnp.maximum(s - 1, 0)]
            keep = jnp.maximum(1 - jnp.maximum(step, 0), 0).astype(F32)
            total = total * keep + products[u]
            tiles[s] = total.astype(BF)
        acc[...] = total
        return carry

    lax.fori_loop(0, SLOTS // STEP, accumulate, 0)

    def emit(buffer, owner_core, j, received):
        def body(q, carry):
            xx, yy = q // YN, q % YN
            first = (yy * 4 + xx * 2 + owner_core) * (NODE // TILE) + j * (PROWS // TILE)
            for g in range(PROWS // TILE):
                end = ends[first + g + 1]
                found = jnp.minimum(end - ends[first + g], 1).astype(F32)
                total = tiles[jnp.maximum(end - 1, 0)] * jnp.full((TILE, FEAT), found, F32).astype(BF)
                rows = pl.ds(pl.multiple_of(q * PROWS + g * TILE, TILE), TILE)
                if received is not None:
                    total = total + received[j, rows, :]
                buffer[j, rows, :] = total
            return carry

        lax.fori_loop(0, 2 * YN, body, 0, unroll=4)

    given = []

    def hand_over(j):
        emit(give, 1 - core, j, None)
        given.append(start(give.at[j], got.at[j], sibling))

    def chunk(xx, yy):
        return (xx * YN + yy) * PROWS

    def at(ref, first, n):
        return ref.at[pl.ds(pl.multiple_of(first, 64), n)]

    up, down, far = (y + 1) % YN, (y + YN - 1) % YN, (y + 2) % YN
    h = PROWS // 2
    state = [None] * PIECES
    slot = {j: n for kind in (False, True) for n, j in enumerate([k for k in range(PIECES) if X_FIRST[k] == kind])}
    def finish_a(j):
        given[j].wait_recv()
        sums, land = mine.at[j], slot[j]
        emit(mine, core, j, got)
        if X_FIRST[j]:
            state[j] = start(at(sums, chunk(1 - xhi, 0), YN * PROWS), x_in.at[land], x_far)
        else:
            into = y_in.at[land]
            state[j] = [
                start(at(sums, chunk(0, far), PROWS), at(into, 0, PROWS), y_next[1]),
                start(at(sums, chunk(1, far), PROWS), at(into, PROWS, PROWS), y_next[-1]),
                start(at(sums, chunk(1, up), PROWS), at(into, 2 * PROWS, PROWS), y_next[1]),
                start(at(sums, chunk(0, down), PROWS), at(into, 3 * PROWS, PROWS), y_next[-1]),
            ]

    def stage_b(j):
        sums, land = mine.at[j], slot[j]
        if X_FIRST[j]:
            state[j].wait_recv()
            into, base = xy_in.at[land], chunk(xhi, 0)
            add_rows(sums, base, [(sums, base), (x_in.at[land], 0)], YN * PROWS)
            state[j] = [
                start(at(sums, chunk(xhi, far), h), at(into, 0, h), y_next[1]),
                start(at(sums, chunk(xhi, far) + h, h), at(into, h, h), y_next[-1]),
                start(at(sums, chunk(xhi, up) + h, h), at(into, 2 * h, h), y_next[1]),
                start(at(sums, chunk(xhi, down), h), at(into, 3 * h, h), y_next[-1]),
            ]
        else:
            into = y_in.at[land]
            state[j][0].wait_recv()
            add_rows(sums, chunk(0, up), [(sums, chunk(0, up)), (into, 0)], PROWS)
            state[j].append(start(at(sums, chunk(0, up), PROWS), at(into, 4 * PROWS, PROWS), y_next[1]))
            state[j][1].wait_recv()
            add_rows(sums, chunk(1, down), [(sums, chunk(1, down)), (into, PROWS)], PROWS)
            state[j].append(start(at(sums, chunk(1, down), PROWS), at(into, 5 * PROWS, PROWS), y_next[-1]))

    def stage_c(j):
        sums, land = mine.at[j], slot[j]
        if X_FIRST[j]:
            into = xy_in.at[land]
            state[j][0].wait_recv()
            add_rows(sums, chunk(xhi, up), [(sums, chunk(xhi, up)), (into, 0)], h)
            state[j].append(start(at(sums, chunk(xhi, up), h), at(into, 4 * h, h), y_next[1]))
            state[j][1].wait_recv()
            add_rows(sums, chunk(xhi, down) + h, [(sums, chunk(xhi, down) + h), (into, h)], h)
            state[j].append(start(at(sums, chunk(xhi, down) + h, h), at(into, 5 * h, h), y_next[-1]))
        else:
            into = y_in.at[land]
            for copy in state[j][2:]:
                copy.wait_recv()
            low = (4, 3)
            high = (2, 5)
            for xx, (one, two) in ((0, low), (1, high)):
                add_rows(
                    sums, chunk(xx, y), [(sums, chunk(xx, y)), (into, one * PROWS), (into, two * PROWS)], PROWS
                )
            state[j] = start(at(sums, chunk(1 - xhi, y), PROWS), yx_in.at[land], x_far)

    def stage_d(j):
        sums, land = mine.at[j], slot[j]
        if X_FIRST[j]:
            into, base = xy_in.at[land], chunk(xhi, y)
            for copy in state[j][2:]:
                copy.wait_recv()
            add_rows(out, j * PROWS, [(sums, base), (into, 4 * h), (into, 3 * h)], h, relu)
            add_rows(out, j * PROWS + h, [(sums, base + h), (into, 2 * h), (into, 5 * h)], h, relu)
        else:
            state[j].wait_recv()
            add_rows(out, j * PROWS, [(sums, chunk(xhi, y)), (yx_in.at[land], 0)], PROWS, relu)

    relu = lambda v: jnp.maximum(v, 0.0)
    stages = {"a": finish_a, "b": stage_b, "c": stage_c, "d": stage_d}
    steps = [("a", j) for j in FIRSTS] + [(stage, j) for stage in "bcd" for j in LATER]
    handed = 0
    for stage, j in steps:
        if stage == "a":
            while handed < min(FIRSTS.index(j) + 1 + AHEAD, PIECES):
                hand_over(FIRSTS[handed])
                handed += 1
        stages[stage](j)
    for copy in copies:
        copy.wait_send()


def local(features, weight, tile_row, tile_col, tile_count, edge_row, edge_col, edge_weight):
    smem = pl.BlockSpec(memory_space=pltpu.SMEM)
    vmem = pl.BlockSpec(memory_space=pltpu.VMEM)
    n_y, n_x = X_FIRST.count(False), X_FIRST.count(True)
    copies = 64 + 8 * PIECES
    return pl.pallas_call(
        layer_kernel,
        out_shape=jax.ShapeDtypeStruct((NODE, FEAT), BF),
        in_specs=[smem] * 3 + [vmem] * 5,
        out_specs=vmem,
        scratch_shapes=[
            pltpu.VMEM((16 * NT, TILE, FEAT), BF),
            pltpu.VMEM((SLOTS, TILE, FEAT), BF),
            pltpu.VMEM((HALF, 128), F32),
            pltpu.VMEM((HALF, 128), F32),
            pltpu.VMEM((HALF, 128), F32),
            pltpu.VMEM((TILE, FEAT), F32),
            pltpu.VMEM((PIECES, 2 * YN * PROWS, FEAT), BF),
            pltpu.VMEM((PIECES, 2 * YN * PROWS, FEAT), BF),
            pltpu.VMEM((PIECES, 2 * YN * PROWS, FEAT), BF),
            pltpu.VMEM((n_y, 6 * PROWS, FEAT), BF),
            pltpu.VMEM((n_y, PROWS, FEAT), BF),
            pltpu.VMEM((n_x, 3 * PROWS, FEAT), BF),
            pltpu.VMEM((n_x, YN * PROWS, FEAT), BF),
            pltpu.SMEM((ENDS,), jnp.int32),
            pltpu.SemaphoreType.DMA((copies,)),
            pltpu.SemaphoreType.DMA((copies,)),
        ],
        compiler_params=pltpu.CompilerParams(
            collective_id=0, has_side_effects=True, vmem_limit_bytes=62 * MIB
        ),
        cost_estimate=pl.CostEstimate(flops=9 * 10**9, bytes_accessed=4 * MIB, transcendentals=0),
        name="graph_layer",
    )(tile_row, tile_col, tile_count, features, weight, edge_row.T, edge_col.T, edge_weight.T)


def solution(mesh):
    in_specs = (
        P(("col", "row"), None),
        P(),
        P(("row", "col")),
        P(("row", "col")),
        P(("row", "col")),
        P(("row", "col"), None),
        P(("row", "col"), None),
        P(("row", "col"), None),
    )
    out_specs = P(("row", "col"), None)
    return jax.shard_map(local, mesh=mesh, in_specs=in_specs, out_specs=out_specs, check_vma=False)
```

```python
import jax
import jax.numpy as jnp
from jax import lax
from jax.experimental import pallas as pl
from jax.experimental.pallas import tpu as pltpu
from jax.sharding import PartitionSpec as P

MESH = pl.DeviceIdType.MESH
BF, F32 = jnp.bfloat16, jnp.float32

TILE = 128
FEAT = 128
NODE = 2048
SLOTS = 1024
ENDS = 260
HALF = SLOTS // 2
EDGES = 64
ZN, YN = 8, 4
NT = NODE // TILE
EARLY = 7
LATE = NT - EARLY
HALVES = {1: (EARLY, LATE // 2), -1: (EARLY + LATE // 2, LATE - LATE // 2)}
PIECES = 8
PT = NT // PIECES
CHUNKS = 2 * YN * PT
X_FIRST = (True, False, True, False, True, False, False, False)
AHEAD = 2
FIRSTS = (0, 1, 2, 3, 4, 5, 6, 7)
LATER = (1, 3, 5, 6, 7, 0, 2, 4)
MIB = 2**20


def place():
    row, col = lax.axis_index("row"), lax.axis_index("col")
    return row // ZN, row % ZN, col // 4, (col // 2) % 2, col % 2


def device(xlo, z, y, xhi, core):
    return (xlo * ZN + z, y * 4 + xhi * 2 + core)


def add_tiles(dst, dst_tile, parts, tiles, finish=None):
    step = min(tiles, 4)

    def body(i, carry):
        total = None
        for ref, first in parts:
            term = ref[pl.ds(first + i * step, step)].astype(F32)
            total = term if total is None else total + term
        if finish is not None:
            total = finish(total)
        dst[pl.ds(dst_tile + i * step, step)] = total.astype(BF)
        return carry

    lax.fori_loop(0, tiles // step, body, 0)


def layer_kernel(
    tile_row, tile_col, count_ref,
    feat, weight, edge_row, edge_col, edge_weight,
    out,
    x, tiles, er2, ec2, ew2, acc, got,
    y_in, yx_in, xy_in, x_in,
    ends, send, recv,
):
    xlo, z, y, xhi, core = place()
    z_next = {1: device(xlo, (z + 1) % ZN, y, xhi, core), -1: device(xlo, (z + ZN - 1) % ZN, y, xhi, core)}
    y_next = {1: device(xlo, z, (y + 1) % YN, xhi, core), -1: device(xlo, z, (y + YN - 1) % YN, xhi, core)}
    x_pair = device(1 - xlo, z, y, xhi, core)
    x_far = device(xlo, z, y, 1 - xhi, core)
    sibling = device(xlo, z, y, xhi, 1 - core)

    barrier = pltpu.get_barrier_semaphore()
    others = [z_next[1], z_next[-1], y_next[1], y_next[-1], x_pair, x_far, sibling]
    for other in others:
        pl.semaphore_signal(barrier, inc=1, device_id=other, device_id_type=MESH)

    copies = []

    def start(src, dst, target):
        number = len(copies)
        copy = pltpu.make_async_remote_copy(
            src_ref=src, dst_ref=dst, send_sem=send.at[number], recv_sem=recv.at[number],
            device_id=target, device_id_type=MESH,
        )
        copy.start()
        copies.append(copy)
        return copy

    def block(i, zz):
        return (i * ZN + zz) * NT

    own = block(xlo, z)

    def transform(i, carry):
        rows = pl.ds(pl.multiple_of(i * 256, 256), 256)
        part = jnp.dot(feat[rows, :], weight[...], preferred_element_type=F32).astype(BF)
        x[pl.ds(own + i * 2, 2)] = part.reshape(2, TILE, FEAT)
        return carry

    lax.fori_loop(0, NODE // 256, transform, 0)

    def prep(i, carry):
        rows = pl.ds(pl.multiple_of(i * 128, 128), 128)

        def both(ref):
            first = ref[:, pl.ds(pl.multiple_of(i * 128, 128), 128)].astype(F32)
            later = ref[:, pl.ds(pl.multiple_of(i * 128 + HALF, 128), 128)].astype(F32)
            return first, later

        first, later = both(edge_row)
        er2[rows, :] = jnp.concatenate([first, later], axis=0).T
        first, later = both(edge_col)
        ec2[rows, :] = jnp.concatenate([first, later + 128.0], axis=0).T
        first, later = both(edge_weight)
        ew2[rows, :] = jnp.concatenate([first, later], axis=0).T
        return carry

    iota = lax.broadcasted_iota(jnp.int32, (256, 128), 0).astype(F32).astype(BF)
    GROUP = 4

    def build(i, carry):
        for u in range(GROUP):
            p = i * GROUP + u

            def spread(ref, n):
                return jnp.concatenate([jnp.broadcast_to(ref[pl.ds(p, 1), :], (16, 128)).astype(BF)] * n, axis=0)

            picks = jnp.where(spread(er2, 8) == iota[:128], spread(ew2, 8), jnp.zeros((128, 128), BF))
            sources = jnp.where(spread(ec2, 16) == iota, jnp.ones((256, 128), BF), jnp.zeros((256, 128), BF))
            dense = lax.dot_general(picks, sources, (((1,), (1,)), ((), ())), preferred_element_type=F32).astype(BF)
            tiles[p] = dense[:, :128]
            tiles[p + HALF] = dense[:, 128:]
        return carry

    count = count_ref[0]
    ROWS_AT_ONCE = 4

    def unit(v):
        return jnp.minimum(jnp.maximum(v, 0), 1)

    def bisect(i, carry):
        rows = [i * ROWS_AT_ONCE + u for u in range(ROWS_AT_ONCE)]
        found = [i * 0 for row in rows]
        for step in (512, 256, 128, 64, 32, 16, 8, 4, 2, 1, 1):
            for u, row in enumerate(rows):
                probe = found[u] + step
                below = unit(row - tile_row[jnp.minimum(probe, SLOTS) - 1])
                found[u] = found[u] + step * below * unit(count + 1 - probe)
        for u, row in enumerate(rows):
            ends[row] = found[u]
        return carry

    bisected = [0]

    def bisect_some(n):
        first = bisected[0]
        lax.fori_loop(first, min(first + n, ENDS // ROWS_AT_ONCE), bisect, 0)
        bisected[0] = min(first + n, ENDS // ROWS_AT_ONCE)

    built = [0]

    def build_some(n):
        first = built[0]
        lax.fori_loop(first, first + n, build, 0)
        built[0] = first + n

    def rows_of(i, zz, offset, n):
        return x.at[pl.ds(block(i, zz) + offset, n)]

    def ring(direction, hop, i, offset, n):
        ref = rows_of(i, (z - direction * (hop - 1) + ZN) % ZN, offset, n)
        return start(ref, ref, z_next[direction])

    def cross(direction, hop, offset, n):
        ref = rows_of(xlo, (z - direction * hop + ZN) % ZN, offset, n)
        return start(ref, ref, x_pair)

    late, early, pair_early = (xlo, EARLY, LATE), (xlo, 0, EARLY), (1 - xlo, 0, EARLY)
    pl.semaphore_wait(barrier, len(others))
    hops = {}
    for d in (1, -1):
        hops[1, d, "late"] = ring(d, 1, *late)
    cross_early = cross(1, 0, 0, EARLY)
    for d in (1, -1):
        hops[1, d, "early"] = ring(d, 1, *early)
    crossed = [cross(1, 0, EARLY, LATE)]
    lax.fori_loop(0, HALF // 128, prep, 0)
    build_some(8)
    cross_early.wait_recv()
    for d in (1, -1):
        hops[1, d, "pair"] = ring(d, 1, *pair_early)
    final = []
    for hop in (1, 2, 3):
        for name, part in (("late", late), ("early", early), ("pair", pair_early)):
            build_some(12)
            bisect_some(8)
            for d in (1, -1):
                hops[hop, d, name].wait_recv()
                if hop < 3:
                    hops[hop + 1, d, name] = ring(d, hop + 1, *part)
                elif name == "late":
                    hops[4, d, name] = ring(d, 4, xlo, *HALVES[d])
                elif (name == "early") == (d == 1):
                    final.append(ring(d, 4, *part))
                if name == "late":
                    crossed.append(cross(d, hop, EARLY, LATE))
    build_some(HALF // GROUP - built[0])
    for d in (1, -1):
        hops[4, d, "late"].wait_recv()
        crossed.append(cross(d, 4, *HALVES[d]))
    for copy in final + crossed:
        copy.wait_recv()

    acc[...] = jnp.zeros_like(acc)
    STEP = 128

    def accumulate(i, carry):
        products = []
        for u in range(STEP):
            s = i * STEP + u
            products.append(jnp.dot(tiles[s], x[tile_col[s]], preferred_element_type=F32))
        total = acc[...]
        for u in range(STEP):
            s = i * STEP + u
            step = tile_row[s] - tile_row[jnp.maximum(s - 1, 0)]
            keep = jnp.maximum(1 - jnp.maximum(step, 0), 0).astype(F32)
            total = total * keep + products[u]
            tiles[s] = total.astype(BF)
        acc[...] = total
        return carry

    lax.fori_loop(0, SLOTS // STEP, accumulate, 0)

    for copy in copies:
        copy.wait_send()
    gathered = len(copies)
    give = [x.at[pl.ds(j * CHUNKS, CHUNKS)] for j in range(PIECES)]
    mine = [x.at[pl.ds((PIECES + j) * CHUNKS, CHUNKS)] for j in range(PIECES)]

    def emit(buffer, owner_core, j, received):
        def body(q, carry):
            xx, yy = q // YN, q % YN
            first = (yy * 4 + xx * 2 + owner_core) * NT + j * PT
            for g in range(PT):
                end = ends[first + g + 1]
                found = jnp.minimum(end - ends[first + g], 1).astype(F32)
                total = tiles[jnp.maximum(end - 1, 0)] * jnp.full((TILE, FEAT), found, F32).astype(BF)
                if received is not None:
                    total = total + received[q * PT + g]
                buffer[q * PT + g] = total
            return carry

        lax.fori_loop(0, 2 * YN, body, 0, unroll=4)

    given = {}

    def hand_over(j):
        emit(give[j], 1 - core, j, None)
        given[j] = start(give[j], got.at[j], sibling)

    def chunk(xx, yy):
        return (xx * YN + yy) * PT

    def at(ref, first, n):
        return ref.at[pl.ds(first, n)]

    up, down, far = (y + 1) % YN, (y + YN - 1) % YN, (y + 2) % YN
    h = PT // 2
    state = [None] * PIECES
    slot = {j: n for kind in (False, True) for n, j in enumerate([k for k in range(PIECES) if X_FIRST[k] == kind])}
    def finish_a(j):
        given[j].wait_recv()
        sums, land = mine[j], slot[j]
        emit(mine[j], core, j, got.at[j])
        if X_FIRST[j]:
            state[j] = start(at(sums, chunk(1 - xhi, 0), YN * PT), x_in.at[land], x_far)
        else:
            into = y_in.at[land]
            state[j] = [
                start(at(sums, chunk(0, far), PT), at(into, 0, PT), y_next[1]),
                start(at(sums, chunk(1, far), PT), at(into, PT, PT), y_next[-1]),
                start(at(sums, chunk(1, up), PT), at(into, 2 * PT, PT), y_next[1]),
                start(at(sums, chunk(0, down), PT), at(into, 3 * PT, PT), y_next[-1]),
            ]

    def stage_b(j):
        sums, land = mine[j], slot[j]
        if X_FIRST[j]:
            state[j].wait_recv()
            into, base = xy_in.at[land], chunk(xhi, 0)
            add_tiles(sums, base, [(sums, base), (x_in.at[land], 0)], YN * PT)
            state[j] = [
                start(at(sums, chunk(xhi, far), h), at(into, 0, h), y_next[1]),
                start(at(sums, chunk(xhi, far) + h, h), at(into, h, h), y_next[-1]),
                start(at(sums, chunk(xhi, up) + h, h), at(into, 2 * h, h), y_next[1]),
                start(at(sums, chunk(xhi, down), h), at(into, 3 * h, h), y_next[-1]),
            ]
        else:
            into = y_in.at[land]
            state[j][0].wait_recv()
            add_tiles(sums, chunk(0, up), [(sums, chunk(0, up)), (into, 0)], PT)
            state[j].append(start(at(sums, chunk(0, up), PT), at(into, 4 * PT, PT), y_next[1]))
            state[j][1].wait_recv()
            add_tiles(sums, chunk(1, down), [(sums, chunk(1, down)), (into, PT)], PT)
            state[j].append(start(at(sums, chunk(1, down), PT), at(into, 5 * PT, PT), y_next[-1]))

    def stage_c(j):
        sums, land = mine[j], slot[j]
        if X_FIRST[j]:
            into = xy_in.at[land]
            state[j][0].wait_recv()
            add_tiles(sums, chunk(xhi, up), [(sums, chunk(xhi, up)), (into, 0)], h)
            state[j].append(start(at(sums, chunk(xhi, up), h), at(into, 4 * h, h), y_next[1]))
            state[j][1].wait_recv()
            add_tiles(sums, chunk(xhi, down) + h, [(sums, chunk(xhi, down) + h), (into, h)], h)
            state[j].append(start(at(sums, chunk(xhi, down) + h, h), at(into, 5 * h, h), y_next[-1]))
        else:
            into = y_in.at[land]
            for copy in state[j][2:]:
                copy.wait_recv()
            low = (4, 3)
            high = (2, 5)
            for xx, (one, two) in ((0, low), (1, high)):
                add_tiles(
                    sums, chunk(xx, y), [(sums, chunk(xx, y)), (into, one * PT), (into, two * PT)], PT
                )
            state[j] = start(at(sums, chunk(1 - xhi, y), PT), yx_in.at[land], x_far)

    def stage_d(j):
        sums, land = mine[j], slot[j]
        if X_FIRST[j]:
            into, base = xy_in.at[land], chunk(xhi, y)
            for copy in state[j][2:]:
                copy.wait_recv()
            add_tiles(out, j * PT, [(sums, base), (into, 4 * h), (into, 3 * h)], h, relu)
            add_tiles(out, j * PT + h, [(sums, base + h), (into, 2 * h), (into, 5 * h)], h, relu)
        else:
            state[j].wait_recv()
            add_tiles(out, j * PT, [(sums, chunk(xhi, y)), (yx_in.at[land], 0)], PT, relu)

    relu = lambda v: jnp.maximum(v, 0.0)
    stages = {"a": finish_a, "b": stage_b, "c": stage_c, "d": stage_d}
    steps = [("a", j) for j in FIRSTS] + [(stage, j) for stage in "bcd" for j in LATER]
    handed = 0
    for stage, j in steps:
        if stage == "a":
            while handed < min(FIRSTS.index(j) + 1 + AHEAD, PIECES):
                hand_over(FIRSTS[handed])
                handed += 1
        stages[stage](j)
    for copy in copies[gathered:]:
        copy.wait_send()


def local(features, weight, tile_row, tile_col, tile_count, edge_row, edge_col, edge_weight):
    smem = pl.BlockSpec(memory_space=pltpu.SMEM)
    vmem = pl.BlockSpec(memory_space=pltpu.VMEM)
    n_y, n_x = X_FIRST.count(False), X_FIRST.count(True)
    copies = 64 + 8 * PIECES
    return pl.pallas_call(
        layer_kernel,
        out_shape=jax.ShapeDtypeStruct((NT, TILE, FEAT), BF),
        in_specs=[smem] * 3 + [vmem] * 5,
        out_specs=vmem,
        scratch_shapes=[
            pltpu.VMEM((16 * NT, TILE, FEAT), BF),
            pltpu.VMEM((SLOTS, TILE, FEAT), BF),
            pltpu.VMEM((HALF, 128), F32),
            pltpu.VMEM((HALF, 128), F32),
            pltpu.VMEM((HALF, 128), F32),
            pltpu.VMEM((TILE, FEAT), F32),
            pltpu.VMEM((PIECES, CHUNKS, TILE, FEAT), BF),
            pltpu.VMEM((n_y, 6 * PT, TILE, FEAT), BF),
            pltpu.VMEM((n_y, PT, TILE, FEAT), BF),
            pltpu.VMEM((n_x, 3 * PT, TILE, FEAT), BF),
            pltpu.VMEM((n_x, YN * PT, TILE, FEAT), BF),
            pltpu.SMEM((ENDS,), jnp.int32),
            pltpu.SemaphoreType.DMA((copies,)),
            pltpu.SemaphoreType.DMA((copies,)),
        ],
        compiler_params=pltpu.CompilerParams(
            collective_id=0, has_side_effects=True, vmem_limit_bytes=62 * MIB
        ),
        cost_estimate=pl.CostEstimate(flops=9 * 10**9, bytes_accessed=4 * MIB, transcendentals=0),
        name="graph_layer",
    )(tile_row, tile_col, tile_count, features, weight, edge_row.T, edge_col.T, edge_weight.T).reshape(NODE, FEAT)


def solution(mesh):
    in_specs = (
        P(("col", "row"), None),
        P(),
        P(("row", "col")),
        P(("row", "col")),
        P(("row", "col")),
        P(("row", "col"), None),
        P(("row", "col"), None),
        P(("row", "col"), None),
    )
    out_specs = P(("row", "col"), None)
    return jax.shard_map(local, mesh=mesh, in_specs=in_specs, out_specs=out_specs, check_vma=False)
```

```python
import jax
import jax.numpy as jnp
from jax import lax
from jax.experimental import pallas as pl
from jax.experimental.pallas import tpu as pltpu
from jax.sharding import PartitionSpec as P

MESH = pl.DeviceIdType.MESH
BF, F32 = jnp.bfloat16, jnp.float32

TILE = 128
FEAT = 128
NODE = 2048
SLOTS = 1024
ENDS = 260
HALF = SLOTS // 2
EDGES = 64
ZN, YN = 8, 4
NT = NODE // TILE
EARLY = 7
LATE = NT - EARLY
HALVES = {1: (EARLY, LATE // 2), -1: (EARLY + LATE // 2, LATE - LATE // 2)}
BUILDS, BISECTS = 11, 7
SERVICES = ((1, "late"), (1, "early"), (2, "late"), (1, "pair"), (2, "early"), (3, "late"), (2, "pair"), (4, "late"), (3, "early"), (3, "pair"))
PIECES = 8
PT = NT // PIECES
CHUNKS = 2 * YN * PT
X_FIRST = (True, False, True, False, True, False, False, False)
AHEAD = 2
FIRSTS = (0, 1, 2, 3, 4, 5, 6, 7)
LATER = (1, 3, 5, 6, 7, 0, 2, 4)
MIB = 2**20


def place():
    row, col = lax.axis_index("row"), lax.axis_index("col")
    return row // ZN, row % ZN, col // 4, (col // 2) % 2, col % 2


def device(xlo, z, y, xhi, core):
    return (xlo * ZN + z, y * 4 + xhi * 2 + core)


def add_tiles(dst, dst_tile, parts, tiles, finish=None):
    step = min(tiles, 4)

    def body(i, carry):
        total = None
        for ref, first in parts:
            term = ref[pl.ds(first + i * step, step)].astype(F32)
            total = term if total is None else total + term
        if finish is not None:
            total = finish(total)
        dst[pl.ds(dst_tile + i * step, step)] = total.astype(BF)
        return carry

    lax.fori_loop(0, tiles // step, body, 0)


def layer_kernel(
    tile_row, tile_col, count_ref,
    feat, weight, edge_row, edge_col, edge_weight,
    out,
    x, tiles, er2, ec2, ew2, acc, got,
    y_in, yx_in, xy_in, x_in,
    ends, send, recv,
):
    xlo, z, y, xhi, core = place()
    z_next = {1: device(xlo, (z + 1) % ZN, y, xhi, core), -1: device(xlo, (z + ZN - 1) % ZN, y, xhi, core)}
    y_next = {1: device(xlo, z, (y + 1) % YN, xhi, core), -1: device(xlo, z, (y + YN - 1) % YN, xhi, core)}
    x_pair = device(1 - xlo, z, y, xhi, core)
    x_far = device(xlo, z, y, 1 - xhi, core)
    sibling = device(xlo, z, y, xhi, 1 - core)

    barrier = pltpu.get_barrier_semaphore()
    others = [z_next[1], z_next[-1], y_next[1], y_next[-1], x_pair, x_far, sibling]
    for other in others:
        pl.semaphore_signal(barrier, inc=1, device_id=other, device_id_type=MESH)

    copies = []

    def start(src, dst, target):
        number = len(copies)
        copy = pltpu.make_async_remote_copy(
            src_ref=src, dst_ref=dst, send_sem=send.at[number], recv_sem=recv.at[number],
            device_id=target, device_id_type=MESH,
        )
        copy.start()
        copies.append(copy)
        return copy

    def block(i, zz):
        return (i * ZN + zz) * NT

    own = block(xlo, z)

    def transform(i, carry):
        rows = pl.ds(pl.multiple_of(i * 256, 256), 256)
        part = jnp.dot(feat[rows, :], weight[...], preferred_element_type=F32).astype(BF)
        x[pl.ds(own + i * 2, 2)] = part.reshape(2, TILE, FEAT)
        return carry

    lax.fori_loop(0, NODE // 256, transform, 0)

    def prep(i, carry):
        rows = pl.ds(pl.multiple_of(i * 128, 128), 128)

        def both(ref):
            first = ref[:, pl.ds(pl.multiple_of(i * 128, 128), 128)].astype(F32)
            later = ref[:, pl.ds(pl.multiple_of(i * 128 + HALF, 128), 128)].astype(F32)
            return first, later

        first, later = both(edge_row)
        er2[rows, :] = jnp.concatenate([first, later], axis=0).T
        first, later = both(edge_col)
        ec2[rows, :] = jnp.concatenate([first, later + 128.0], axis=0).T
        first, later = both(edge_weight)
        ew2[rows, :] = jnp.concatenate([first, later], axis=0).T
        return carry

    iota = lax.broadcasted_iota(jnp.int32, (256, 128), 0).astype(F32).astype(BF)
    GROUP = 4

    def build(i, carry):
        for u in range(GROUP):
            p = i * GROUP + u

            def spread(ref, n):
                return jnp.concatenate([jnp.broadcast_to(ref[pl.ds(p, 1), :], (16, 128)).astype(BF)] * n, axis=0)

            picks = jnp.where(spread(er2, 8) == iota[:128], spread(ew2, 8), jnp.zeros((128, 128), BF))
            sources = jnp.where(spread(ec2, 16) == iota, jnp.ones((256, 128), BF), jnp.zeros((256, 128), BF))
            dense = lax.dot_general(picks, sources, (((1,), (1,)), ((), ())), preferred_element_type=F32).astype(BF)
            tiles[p] = dense[:, :128]
            tiles[p + HALF] = dense[:, 128:]
        return carry

    count = count_ref[0]
    ROWS_AT_ONCE = 4

    def unit(v):
        return jnp.minimum(jnp.maximum(v, 0), 1)

    def bisect(i, carry):
        rows = [i * ROWS_AT_ONCE + u for u in range(ROWS_AT_ONCE)]
        found = [i * 0 for row in rows]
        for step in (512, 256, 128, 64, 32, 16, 8, 4, 2, 1, 1):
            for u, row in enumerate(rows):
                probe = found[u] + step
                below = unit(row - tile_row[jnp.minimum(probe, SLOTS) - 1])
                found[u] = found[u] + step * below * unit(count + 1 - probe)
        for u, row in enumerate(rows):
            ends[row] = found[u]
        return carry

    bisected = [0]

    def bisect_some(n):
        first = bisected[0]
        lax.fori_loop(first, min(first + n, ENDS // ROWS_AT_ONCE), bisect, 0)
        bisected[0] = min(first + n, ENDS // ROWS_AT_ONCE)

    built = [0]

    def build_some(n):
        first = built[0]
        lax.fori_loop(first, first + n, build, 0)
        built[0] = first + n

    def rows_of(i, zz, offset, n):
        return x.at[pl.ds(block(i, zz) + offset, n)]

    def ring(direction, hop, i, offset, n):
        ref = rows_of(i, (z - direction * (hop - 1) + ZN) % ZN, offset, n)
        return start(ref, ref, z_next[direction])

    def cross(direction, hop, offset, n):
        ref = rows_of(xlo, (z - direction * hop + ZN) % ZN, offset, n)
        return start(ref, ref, x_pair)

    late, early, pair_early = (xlo, EARLY, LATE), (xlo, 0, EARLY), (1 - xlo, 0, EARLY)
    pl.semaphore_wait(barrier, len(others))
    hops = {}
    for d in (1, -1):
        hops[1, d, "late"] = ring(d, 1, *late)
    cross_early = cross(1, 0, 0, EARLY)
    for d in (1, -1):
        hops[1, d, "early"] = ring(d, 1, *early)
    crossed = [cross(1, 0, EARLY, LATE)]
    lax.fori_loop(0, HALF // 128, prep, 0)
    build_some(8)
    cross_early.wait_recv()
    for d in (1, -1):
        hops[1, d, "pair"] = ring(d, 1, *pair_early)
    final = []
    parts = {"late": late, "early": early, "pair": pair_early}
    for hop, name in SERVICES:
        build_some(BUILDS)
        bisect_some(BISECTS)
        for d in (1, -1):
            hops[hop, d, name].wait_recv()
            if hop < 3:
                hops[hop + 1, d, name] = ring(d, hop + 1, *parts[name])
            elif hop == 3 and name == "late":
                hops[4, d, name] = ring(d, 4, xlo, *HALVES[d])
            elif (name == "early") == (d == 1) and name != "late":
                final.append(ring(d, 4, *parts[name]))
            if name == "late":
                crossed.append(cross(d, hop, *((EARLY, LATE) if hop < 4 else HALVES[d])))
    build_some(HALF // GROUP - built[0])
    for copy in final + crossed:
        copy.wait_recv()

    acc[...] = jnp.zeros_like(acc)
    STEP = 128

    def accumulate(i, carry):
        products = []
        for u in range(STEP):
            s = i * STEP + u
            products.append(jnp.dot(tiles[s], x[tile_col[s]], preferred_element_type=F32))
        total = acc[...]
        for u in range(STEP):
            s = i * STEP + u
            step = tile_row[s] - tile_row[jnp.maximum(s - 1, 0)]
            keep = jnp.maximum(1 - jnp.maximum(step, 0), 0).astype(F32)
            total = total * keep + products[u]
            tiles[s] = total.astype(BF)
        acc[...] = total
        return carry

    lax.fori_loop(0, SLOTS // STEP, accumulate, 0)

    for copy in copies:
        copy.wait_send()
    gathered = len(copies)
    give = [x.at[pl.ds(j * CHUNKS, CHUNKS)] for j in range(PIECES)]
    mine = [x.at[pl.ds((PIECES + j) * CHUNKS, CHUNKS)] for j in range(PIECES)]

    def emit(buffer, owner_core, j, received):
        def body(q, carry):
            xx, yy = q // YN, q % YN
            first = (yy * 4 + xx * 2 + owner_core) * NT + j * PT
            for g in range(PT):
                end = ends[first + g + 1]
                found = jnp.minimum(end - ends[first + g], 1).astype(F32)
                total = tiles[jnp.maximum(end - 1, 0)] * jnp.full((TILE, FEAT), found, F32).astype(BF)
                if received is not None:
                    total = total + received[q * PT + g]
                buffer[q * PT + g] = total
            return carry

        lax.fori_loop(0, 2 * YN, body, 0, unroll=4)

    given = {}

    def hand_over(j):
        emit(give[j], 1 - core, j, None)
        given[j] = start(give[j], got.at[j], sibling)

    def chunk(xx, yy):
        return (xx * YN + yy) * PT

    def at(ref, first, n):
        return ref.at[pl.ds(first, n)]

    up, down, far = (y + 1) % YN, (y + YN - 1) % YN, (y + 2) % YN
    h = PT // 2
    state = [None] * PIECES
    slot = {j: n for kind in (False, True) for n, j in enumerate([k for k in range(PIECES) if X_FIRST[k] == kind])}
    def finish_a(j):
        given[j].wait_recv()
        sums, land = mine[j], slot[j]
        emit(mine[j], core, j, got.at[j])
        if X_FIRST[j]:
            state[j] = start(at(sums, chunk(1 - xhi, 0), YN * PT), x_in.at[land], x_far)
        else:
            into = y_in.at[land]
            state[j] = [
                start(at(sums, chunk(0, far), PT), at(into, 0, PT), y_next[1]),
                start(at(sums, chunk(1, far), PT), at(into, PT, PT), y_next[-1]),
                start(at(sums, chunk(1, up), PT), at(into, 2 * PT, PT), y_next[1]),
                start(at(sums, chunk(0, down), PT), at(into, 3 * PT, PT), y_next[-1]),
            ]

    def stage_b(j):
        sums, land = mine[j], slot[j]
        if X_FIRST[j]:
            state[j].wait_recv()
            into, base = xy_in.at[land], chunk(xhi, 0)
            add_tiles(sums, base, [(sums, base), (x_in.at[land], 0)], YN * PT)
            state[j] = [
                start(at(sums, chunk(xhi, far), h), at(into, 0, h), y_next[1]),
                start(at(sums, chunk(xhi, far) + h, h), at(into, h, h), y_next[-1]),
                start(at(sums, chunk(xhi, up) + h, h), at(into, 2 * h, h), y_next[1]),
                start(at(sums, chunk(xhi, down), h), at(into, 3 * h, h), y_next[-1]),
            ]
        else:
            into = y_in.at[land]
            state[j][0].wait_recv()
            add_tiles(sums, chunk(0, up), [(sums, chunk(0, up)), (into, 0)], PT)
            state[j].append(start(at(sums, chunk(0, up), PT), at(into, 4 * PT, PT), y_next[1]))
            state[j][1].wait_recv()
            add_tiles(sums, chunk(1, down), [(sums, chunk(1, down)), (into, PT)], PT)
            state[j].append(start(at(sums, chunk(1, down), PT), at(into, 5 * PT, PT), y_next[-1]))

    def stage_c(j):
        sums, land = mine[j], slot[j]
        if X_FIRST[j]:
            into = xy_in.at[land]
            state[j][0].wait_recv()
            add_tiles(sums, chunk(xhi, up), [(sums, chunk(xhi, up)), (into, 0)], h)
            state[j].append(start(at(sums, chunk(xhi, up), h), at(into, 4 * h, h), y_next[1]))
            state[j][1].wait_recv()
            add_tiles(sums, chunk(xhi, down) + h, [(sums, chunk(xhi, down) + h), (into, h)], h)
            state[j].append(start(at(sums, chunk(xhi, down) + h, h), at(into, 5 * h, h), y_next[-1]))
        else:
            into = y_in.at[land]
            for copy in state[j][2:]:
                copy.wait_recv()
            low = (4, 3)
            high = (2, 5)
            for xx, (one, two) in ((0, low), (1, high)):
                add_tiles(
                    sums, chunk(xx, y), [(sums, chunk(xx, y)), (into, one * PT), (into, two * PT)], PT
                )
            state[j] = start(at(sums, chunk(1 - xhi, y), PT), yx_in.at[land], x_far)

    def stage_d(j):
        sums, land = mine[j], slot[j]
        if X_FIRST[j]:
            into, base = xy_in.at[land], chunk(xhi, y)
            for copy in state[j][2:]:
                copy.wait_recv()
            add_tiles(out, j * PT, [(sums, base), (into, 4 * h), (into, 3 * h)], h, relu)
            add_tiles(out, j * PT + h, [(sums, base + h), (into, 2 * h), (into, 5 * h)], h, relu)
        else:
            state[j].wait_recv()
            add_tiles(out, j * PT, [(sums, chunk(xhi, y)), (yx_in.at[land], 0)], PT, relu)

    relu = lambda v: jnp.maximum(v, 0.0)
    stages = {"a": finish_a, "b": stage_b, "c": stage_c, "d": stage_d}
    steps = [("a", j) for j in FIRSTS] + [(stage, j) for stage in "bcd" for j in LATER]
    handed = 0
    for stage, j in steps:
        if stage == "a":
            while handed < min(FIRSTS.index(j) + 1 + AHEAD, PIECES):
                hand_over(FIRSTS[handed])
                handed += 1
        stages[stage](j)
    for copy in copies[gathered:]:
        copy.wait_send()


def local(features, weight, tile_row, tile_col, tile_count, edge_row, edge_col, edge_weight):
    smem = pl.BlockSpec(memory_space=pltpu.SMEM)
    vmem = pl.BlockSpec(memory_space=pltpu.VMEM)
    n_y, n_x = X_FIRST.count(False), X_FIRST.count(True)
    copies = 64 + 8 * PIECES
    return pl.pallas_call(
        layer_kernel,
        out_shape=jax.ShapeDtypeStruct((NT, TILE, FEAT), BF),
        in_specs=[smem] * 3 + [vmem] * 5,
        out_specs=vmem,
        scratch_shapes=[
            pltpu.VMEM((16 * NT, TILE, FEAT), BF),
            pltpu.VMEM((SLOTS, TILE, FEAT), BF),
            pltpu.VMEM((HALF, 128), F32),
            pltpu.VMEM((HALF, 128), F32),
            pltpu.VMEM((HALF, 128), F32),
            pltpu.VMEM((TILE, FEAT), F32),
            pltpu.VMEM((PIECES, CHUNKS, TILE, FEAT), BF),
            pltpu.VMEM((n_y, 6 * PT, TILE, FEAT), BF),
            pltpu.VMEM((n_y, PT, TILE, FEAT), BF),
            pltpu.VMEM((n_x, 3 * PT, TILE, FEAT), BF),
            pltpu.VMEM((n_x, YN * PT, TILE, FEAT), BF),
            pltpu.SMEM((ENDS,), jnp.int32),
            pltpu.SemaphoreType.DMA((copies,)),
            pltpu.SemaphoreType.DMA((copies,)),
        ],
        compiler_params=pltpu.CompilerParams(
            collective_id=0, has_side_effects=True, vmem_limit_bytes=62 * MIB
        ),
        cost_estimate=pl.CostEstimate(flops=9 * 10**9, bytes_accessed=4 * MIB, transcendentals=0),
        name="graph_layer",
    )(tile_row, tile_col, tile_count, features, weight, edge_row.T, edge_col.T, edge_weight.T).reshape(NODE, FEAT)


def solution(mesh):
    in_specs = (
        P(("col", "row"), None),
        P(),
        P(("row", "col")),
        P(("row", "col")),
        P(("row", "col")),
        P(("row", "col"), None),
        P(("row", "col"), None),
        P(("row", "col"), None),
    )
    out_specs = P(("row", "col"), None)
    return jax.shard_map(local, mesh=mesh, in_specs=in_specs, out_specs=out_specs, check_vma=False)
```

```python
import jax
import jax.numpy as jnp
from jax import lax
from jax.experimental import pallas as pl
from jax.experimental.pallas import tpu as pltpu
from jax.sharding import PartitionSpec as P

MESH = pl.DeviceIdType.MESH
BF, F32 = jnp.bfloat16, jnp.float32

TILE = 128
FEAT = 128
NODE = 2048
SLOTS = 1024
ENDS = 260
HALF = SLOTS // 2
EDGES = 64
ZN, YN = 8, 4
NT = NODE // TILE
EARLY = 7
LATE = NT - EARLY
HALVES = {1: (EARLY, LATE // 2), -1: (EARLY + LATE // 2, LATE - LATE // 2)}
BUILDS, BISECTS = 9, 7
SERVICES = ((1, "late"), (1, "early"), (2, "late"), (1, "pair"), (2, "early"), (3, "late"), (2, "pair"), (4, "late"), (3, "early"), (3, "pair"))
PIECES = 8
PT = NT // PIECES
CHUNKS = 2 * YN * PT
X_FIRST = (True, False, True, False, True, False, False, False)
AHEAD = 2
FIRSTS = (0, 1, 2, 3, 4, 5, 6, 7)
LATER = (1, 3, 5, 6, 7, 0, 2, 4)
MIB = 2**20


def place():
    row, col = lax.axis_index("row"), lax.axis_index("col")
    return row // ZN, row % ZN, col // 4, (col // 2) % 2, col % 2


def device(xlo, z, y, xhi, core):
    return (xlo * ZN + z, y * 4 + xhi * 2 + core)


def add_tiles(dst, dst_tile, parts, tiles, finish=None):
    step = min(tiles, 4)

    def body(i, carry):
        total = None
        for ref, first in parts:
            term = ref[pl.ds(first + i * step, step)].astype(F32)
            total = term if total is None else total + term
        if finish is not None:
            total = finish(total)
        dst[pl.ds(dst_tile + i * step, step)] = total.astype(BF)
        return carry

    lax.fori_loop(0, tiles // step, body, 0)


def layer_kernel(
    tile_row, tile_col, count_ref,
    feat, weight, edge_row, edge_col, edge_weight,
    out,
    x, tiles, er2, ec2, ew2, acc, got,
    y_in, yx_in, xy_in, x_in,
    ends, send, recv,
):
    xlo, z, y, xhi, core = place()
    z_next = {1: device(xlo, (z + 1) % ZN, y, xhi, core), -1: device(xlo, (z + ZN - 1) % ZN, y, xhi, core)}
    y_next = {1: device(xlo, z, (y + 1) % YN, xhi, core), -1: device(xlo, z, (y + YN - 1) % YN, xhi, core)}
    x_pair = device(1 - xlo, z, y, xhi, core)
    x_far = device(xlo, z, y, 1 - xhi, core)
    sibling = device(xlo, z, y, xhi, 1 - core)

    barrier = pltpu.get_barrier_semaphore()
    others = [z_next[1], z_next[-1], y_next[1], y_next[-1], x_pair, x_far, sibling]
    for other in others:
        pl.semaphore_signal(barrier, inc=1, device_id=other, device_id_type=MESH)

    copies = []

    def start(src, dst, target):
        number = len(copies)
        copy = pltpu.make_async_remote_copy(
            src_ref=src, dst_ref=dst, send_sem=send.at[number], recv_sem=recv.at[number],
            device_id=target, device_id_type=MESH,
        )
        copy.start()
        copies.append(copy)
        return copy

    def block(i, zz):
        return (i * ZN + zz) * NT

    own = block(xlo, z)

    def transform(i, carry):
        rows = pl.ds(pl.multiple_of(i * 256, 256), 256)
        part = jnp.dot(feat[rows, :], weight[...], preferred_element_type=F32).astype(BF)
        x[pl.ds(own + i * 2, 2)] = part.reshape(2, TILE, FEAT)
        return carry

    lax.fori_loop(0, NODE // 256, transform, 0)

    def prep(i, carry):
        rows = pl.ds(pl.multiple_of(i * 128, 128), 128)

        def both(ref):
            first = ref[:, pl.ds(pl.multiple_of(i * 128, 128), 128)].astype(F32)
            later = ref[:, pl.ds(pl.multiple_of(i * 128 + HALF, 128), 128)].astype(F32)
            return first, later

        first, later = both(edge_row)
        er2[rows, :] = jnp.concatenate([first, later], axis=0).T
        first, later = both(edge_col)
        ec2[rows, :] = jnp.concatenate([first, later + 128.0], axis=0).T
        first, later = both(edge_weight)
        ew2[rows, :] = jnp.concatenate([first, later], axis=0).T
        return carry

    iota = lax.broadcasted_iota(jnp.int32, (256, 128), 0).astype(F32).astype(BF)
    GROUP = 4

    def build(i, carry):
        for u in range(GROUP):
            p = i * GROUP + u

            def spread(ref, n):
                return jnp.concatenate([jnp.broadcast_to(ref[pl.ds(p, 1), :], (16, 128)).astype(BF)] * n, axis=0)

            picks = jnp.where(spread(er2, 8) == iota[:128], spread(ew2, 8), jnp.zeros((128, 128), BF))
            sources = jnp.where(spread(ec2, 16) == iota, jnp.ones((256, 128), BF), jnp.zeros((256, 128), BF))
            dense = lax.dot_general(picks, sources, (((1,), (1,)), ((), ())), preferred_element_type=F32).astype(BF)
            tiles[p] = dense[:, :128]
            tiles[p + HALF] = dense[:, 128:]
        return carry

    count = count_ref[0]
    ROWS_AT_ONCE = 4

    def unit(v):
        return jnp.minimum(jnp.maximum(v, 0), 1)

    def bisect(i, carry):
        rows = [i * ROWS_AT_ONCE + u for u in range(ROWS_AT_ONCE)]
        found = [i * 0 for row in rows]
        for step in (512, 256, 128, 64, 32, 16, 8, 4, 2, 1, 1):
            for u, row in enumerate(rows):
                probe = found[u] + step
                below = unit(row - tile_row[jnp.minimum(probe, SLOTS) - 1])
                found[u] = found[u] + step * below * unit(count + 1 - probe)
        for u, row in enumerate(rows):
            ends[row] = found[u]
        return carry

    bisected = [0]

    def bisect_some(n):
        first = bisected[0]
        lax.fori_loop(first, min(first + n, ENDS // ROWS_AT_ONCE), bisect, 0)
        bisected[0] = min(first + n, ENDS // ROWS_AT_ONCE)

    built = [0]

    def build_some(n):
        first = built[0]
        lax.fori_loop(first, first + n, build, 0)
        built[0] = first + n

    def rows_of(i, zz, offset, n):
        return x.at[pl.ds(block(i, zz) + offset, n)]

    def ring(direction, hop, i, offset, n):
        ref = rows_of(i, (z - direction * (hop - 1) + ZN) % ZN, offset, n)
        return start(ref, ref, z_next[direction])

    def cross(direction, hop, offset, n):
        ref = rows_of(xlo, (z - direction * hop + ZN) % ZN, offset, n)
        return start(ref, ref, x_pair)

    late, early, pair_early = (xlo, EARLY, LATE), (xlo, 0, EARLY), (1 - xlo, 0, EARLY)
    pl.semaphore_wait(barrier, len(others))
    hops = {}
    for d in (1, -1):
        hops[1, d, "late"] = ring(d, 1, *late)
    cross_early = cross(1, 0, 0, EARLY)
    for d in (1, -1):
        hops[1, d, "early"] = ring(d, 1, *early)
    crossed = [cross(1, 0, EARLY, LATE)]
    lax.fori_loop(0, HALF // 128, prep, 0)
    build_some(20)
    cross_early.wait_recv()
    for d in (1, -1):
        hops[1, d, "pair"] = ring(d, 1, *pair_early)
    final = []
    parts = {"late": late, "early": early, "pair": pair_early}
    for hop, name in SERVICES:
        build_some(BUILDS)
        bisect_some(BISECTS)
        for d in (1, -1):
            hops[hop, d, name].wait_recv()
            if hop < 3:
                hops[hop + 1, d, name] = ring(d, hop + 1, *parts[name])
            elif hop == 3 and name == "late":
                hops[4, d, name] = ring(d, 4, xlo, *HALVES[d])
            elif (name == "early") == (d == 1) and name != "late":
                final.append(ring(d, 4, *parts[name]))
            if name == "late":
                crossed.append(cross(d, hop, *((EARLY, LATE) if hop < 4 else HALVES[d])))
    build_some(HALF // GROUP - built[0])
    for copy in final + crossed:
        copy.wait_recv()

    acc[...] = jnp.zeros_like(acc)
    STEP = 128

    def accumulate(i, carry):
        products = []
        for u in range(STEP):
            s = i * STEP + u
            products.append(jnp.dot(tiles[s], x[tile_col[s]], preferred_element_type=F32))
        total = acc[...]
        for u in range(STEP):
            s = i * STEP + u
            step = tile_row[s] - tile_row[jnp.maximum(s - 1, 0)]
            keep = jnp.maximum(1 - jnp.maximum(step, 0), 0).astype(F32)
            total = total * keep + products[u]
            tiles[s] = total.astype(BF)
        acc[...] = total
        return carry

    lax.fori_loop(0, SLOTS // STEP, accumulate, 0)

    for copy in copies:
        copy.wait_send()
    gathered = len(copies)
    give = [x.at[pl.ds(j * CHUNKS, CHUNKS)] for j in range(PIECES)]
    mine = [x.at[pl.ds((PIECES + j) * CHUNKS, CHUNKS)] for j in range(PIECES)]

    def emit(buffer, owner_core, j, received):
        def body(q, carry):
            xx, yy = q // YN, q % YN
            first = (yy * 4 + xx * 2 + owner_core) * NT + j * PT
            for g in range(PT):
                end = ends[first + g + 1]
                found = jnp.minimum(end - ends[first + g], 1).astype(F32)
                total = tiles[jnp.maximum(end - 1, 0)] * jnp.full((TILE, FEAT), found, F32).astype(BF)
                if received is not None:
                    total = total + received[q * PT + g]
                buffer[q * PT + g] = total
            return carry

        lax.fori_loop(0, 2 * YN, body, 0, unroll=4)

    given = {}

    def hand_over(j):
        emit(give[j], 1 - core, j, None)
        given[j] = start(give[j], got.at[j], sibling)

    def chunk(xx, yy):
        return (xx * YN + yy) * PT

    def at(ref, first, n):
        return ref.at[pl.ds(first, n)]

    up, down, far = (y + 1) % YN, (y + YN - 1) % YN, (y + 2) % YN
    h = PT // 2
    state = [None] * PIECES
    slot = {j: n for kind in (False, True) for n, j in enumerate([k for k in range(PIECES) if X_FIRST[k] == kind])}
    def finish_a(j):
        given[j].wait_recv()
        sums, land = mine[j], slot[j]
        emit(mine[j], core, j, got.at[j])
        if X_FIRST[j]:
            state[j] = start(at(sums, chunk(1 - xhi, 0), YN * PT), x_in.at[land], x_far)
        else:
            into = y_in.at[land]
            state[j] = [
                start(at(sums, chunk(0, far), PT), at(into, 0, PT), y_next[1]),
                start(at(sums, chunk(1, far), PT), at(into, PT, PT), y_next[-1]),
                start(at(sums, chunk(1, up), PT), at(into, 2 * PT, PT), y_next[1]),
                start(at(sums, chunk(0, down), PT), at(into, 3 * PT, PT), y_next[-1]),
            ]

    def stage_b(j):
        sums, land = mine[j], slot[j]
        if X_FIRST[j]:
            state[j].wait_recv()
            into, base = xy_in.at[land], chunk(xhi, 0)
            add_tiles(sums, base, [(sums, base), (x_in.at[land], 0)], YN * PT)
            state[j] = [
                start(at(sums, chunk(xhi, far), h), at(into, 0, h), y_next[1]),
                start(at(sums, chunk(xhi, far) + h, h), at(into, h, h), y_next[-1]),
                start(at(sums, chunk(xhi, up) + h, h), at(into, 2 * h, h), y_next[1]),
                start(at(sums, chunk(xhi, down), h), at(into, 3 * h, h), y_next[-1]),
            ]
        else:
            into = y_in.at[land]
            state[j][0].wait_recv()
            add_tiles(sums, chunk(0, up), [(sums, chunk(0, up)), (into, 0)], PT)
            state[j].append(start(at(sums, chunk(0, up), PT), at(into, 4 * PT, PT), y_next[1]))
            state[j][1].wait_recv()
            add_tiles(sums, chunk(1, down), [(sums, chunk(1, down)), (into, PT)], PT)
            state[j].append(start(at(sums, chunk(1, down), PT), at(into, 5 * PT, PT), y_next[-1]))

    def stage_c(j):
        sums, land = mine[j], slot[j]
        if X_FIRST[j]:
            into = xy_in.at[land]
            state[j][0].wait_recv()
            add_tiles(sums, chunk(xhi, up), [(sums, chunk(xhi, up)), (into, 0)], h)
            state[j].append(start(at(sums, chunk(xhi, up), h), at(into, 4 * h, h), y_next[1]))
            state[j][1].wait_recv()
            add_tiles(sums, chunk(xhi, down) + h, [(sums, chunk(xhi, down) + h), (into, h)], h)
            state[j].append(start(at(sums, chunk(xhi, down) + h, h), at(into, 5 * h, h), y_next[-1]))
        else:
            into = y_in.at[land]
            for copy in state[j][2:]:
                copy.wait_recv()
            low = (4, 3)
            high = (2, 5)
            for xx, (one, two) in ((0, low), (1, high)):
                add_tiles(
                    sums, chunk(xx, y), [(sums, chunk(xx, y)), (into, one * PT), (into, two * PT)], PT
                )
            state[j] = start(at(sums, chunk(1 - xhi, y), PT), yx_in.at[land], x_far)

    def stage_d(j):
        sums, land = mine[j], slot[j]
        if X_FIRST[j]:
            into, base = xy_in.at[land], chunk(xhi, y)
            for copy in state[j][2:]:
                copy.wait_recv()
            add_tiles(out, j * PT, [(sums, base), (into, 4 * h), (into, 3 * h)], h, relu)
            add_tiles(out, j * PT + h, [(sums, base + h), (into, 2 * h), (into, 5 * h)], h, relu)
        else:
            state[j].wait_recv()
            add_tiles(out, j * PT, [(sums, chunk(xhi, y)), (yx_in.at[land], 0)], PT, relu)

    relu = lambda v: jnp.maximum(v, 0.0)
    stages = {"a": finish_a, "b": stage_b, "c": stage_c, "d": stage_d}
    steps = [("a", j) for j in FIRSTS] + [(stage, j) for stage in "bcd" for j in LATER]
    handed = 0
    for stage, j in steps:
        if stage == "a":
            while handed < min(FIRSTS.index(j) + 1 + AHEAD, PIECES):
                hand_over(FIRSTS[handed])
                handed += 1
        stages[stage](j)
    for copy in copies[gathered:]:
        copy.wait_send()


def local(features, weight, tile_row, tile_col, tile_count, edge_row, edge_col, edge_weight):
    smem = pl.BlockSpec(memory_space=pltpu.SMEM)
    vmem = pl.BlockSpec(memory_space=pltpu.VMEM)
    n_y, n_x = X_FIRST.count(False), X_FIRST.count(True)
    copies = 64 + 8 * PIECES
    return pl.pallas_call(
        layer_kernel,
        out_shape=jax.ShapeDtypeStruct((NT, TILE, FEAT), BF),
        in_specs=[smem] * 3 + [vmem] * 5,
        out_specs=vmem,
        scratch_shapes=[
            pltpu.VMEM((16 * NT, TILE, FEAT), BF),
            pltpu.VMEM((SLOTS, TILE, FEAT), BF),
            pltpu.VMEM((HALF, 128), F32),
            pltpu.VMEM((HALF, 128), F32),
            pltpu.VMEM((HALF, 128), F32),
            pltpu.VMEM((TILE, FEAT), F32),
            pltpu.VMEM((PIECES, CHUNKS, TILE, FEAT), BF),
            pltpu.VMEM((n_y, 6 * PT, TILE, FEAT), BF),
            pltpu.VMEM((n_y, PT, TILE, FEAT), BF),
            pltpu.VMEM((n_x, 3 * PT, TILE, FEAT), BF),
            pltpu.VMEM((n_x, YN * PT, TILE, FEAT), BF),
            pltpu.SMEM((ENDS,), jnp.int32),
            pltpu.SemaphoreType.DMA((copies,)),
            pltpu.SemaphoreType.DMA((copies,)),
        ],
        compiler_params=pltpu.CompilerParams(
            collective_id=0, has_side_effects=True, vmem_limit_bytes=62 * MIB
        ),
        cost_estimate=pl.CostEstimate(flops=9 * 10**9, bytes_accessed=4 * MIB, transcendentals=0),
        name="graph_layer",
    )(tile_row, tile_col, tile_count, features, weight, edge_row.T, edge_col.T, edge_weight.T).reshape(NODE, FEAT)


def solution(mesh):
    in_specs = (
        P(("col", "row"), None),
        P(),
        P(("row", "col")),
        P(("row", "col")),
        P(("row", "col")),
        P(("row", "col"), None),
        P(("row", "col"), None),
        P(("row", "col"), None),
    )
    out_specs = P(("row", "col"), None)
    return jax.shard_map(local, mesh=mesh, in_specs=in_specs, out_specs=out_specs, check_vma=False)
```
